256 devices in a mesh: ax: 16 (over z, core), xs: 16 (over x, y).
Axes of the slice: x: 4, y: 4, z: 8, core: 2. Of those that a mesh axis runs over, the one named last changes fastest.
Arguments:
- scalar: float32 [128, 256, 1024], P('ax', 'xs'), may hold values from 0 to 1
- axial_rate: float32 [128, 256, 1024], P('ax', 'xs'), may hold values from 1.1 to 2.4
- swirl_rate: float32 [128, 256, 1024], P('ax', 'xs'), may hold values from -4 to 4
Outputs:
- transported: float32 [128, 256, 1024], P('ax', 'xs')
The draws below stay inside these ranges and needn't reach their ends.
All inputs are finite; a program needn't handle non-finite values.
Results may differ from the reference program's by a relative error of at most 0.00014.
Values sent between devices are 32-bit elements; how exact they have to be, the bound alone decides.
No kernel may reach another device: no remote copies, remote signals or barrier semaphores. Data moves between devices by JAX's collectives and lax.ppermute only.
A program may use at most 64 MiB of HBM per device.

```python
import math
import jax
import jax.numpy as jnp
from jax import lax

NR = 256
NT = 1024
CZ = 8
SUBSTEPS = 2
NZ = 128


def block_levels(stream_key, dims, shards, least, top_value):
    loudness = 1.0
    for dim, blocks in shards:
        draws = jax.random.uniform(jax.random.fold_in(jax.random.fold_in(stream_key, 6), dim), (blocks,), jnp.float32, least / len(shards), top_value / len(shards))
        loudness = loudness * jnp.repeat(jnp.exp(draws), dims[dim] // blocks).reshape((-1,) + (1,) * (len(dims) - 1 - dim))
    return loudness


def normal_values(rng, extent, deviation, most, pieces=(), kind=jnp.bfloat16):
    values = deviation * jax.random.normal(rng, extent, jnp.float32)
    if pieces:
        values = values * block_levels(rng, extent, pieces, -0.22, 0.18)
    return jnp.clip(values, -most, most).astype(kind)


def setup_inputs(seed: int = 0) -> dict:
    streams_of = jax.random.split(jax.random.key(seed), 4)
    scalar = jnp.clip(1.0 * jax.random.uniform(streams_of[0], (NZ, NR, NT), jnp.float32) ** block_levels(streams_of[0], (NZ, NR, NT), ((0, 16), (1, 16)), -0.2, 0.2), 0.0, 1.0)
    axial_rate = jnp.clip(jnp.exp(math.log(2.4) - 0.7801586 * jax.random.uniform(streams_of[1], (NZ, NR, NT), jnp.float32) ** block_levels(streams_of[1], (NZ, NR, NT), ((0, 16), (1, 16)), -0.2, 0.2)), 1.1, 2.4)
    swirl_rate = normal_values(streams_of[2], (NZ, NR, NT), 1.0, 4.0, ((0, 16), (1, 16)), jnp.float32)
    return {"scalar": scalar, "axial_rate": axial_rate, "swirl_rate": swirl_rate}


axial_weight = 0.2
azimuth_damp = 0.5
diffusion_number = 1.0
stencil_coeffs = (-1.0 / 560.0, 8.0 / 315.0, -0.2, 1.6, -205.0 / 72.0, 1.6, -0.2, 8.0 / 315.0, -1.0 / 560.0)

def radial_bands(cell_count, diffusion_value):
    cell_index = jnp.arange(cell_count, dtype=jnp.float32)
    radius = cell_index + 0.5
    upper_face = jnp.where(cell_index < cell_count - 1, cell_index + 1.0, 0.0)
    sub_diag = -diffusion_value * cell_index / radius
    super_diag = -diffusion_value * upper_face / radius
    main_diag = 1.0 - sub_diag - super_diag
    return (sub_diag, main_diag, super_diag)

def reference(scalar, axial_rate, swirl_rate):
    sub_diag, main_diag, super_diag = radial_bands(NR, diffusion_number)
    band_shape = (NZ, NR)
    sub_full = jnp.broadcast_to(sub_diag, band_shape)
    main_full = jnp.broadcast_to(main_diag, band_shape)
    super_full = jnp.broadcast_to(super_diag, band_shape)
    radius = jnp.arange(NR, dtype=jnp.float32) + 0.5
    nyquist = NT // 2
    wavenum = jnp.arange(nyquist + 1, dtype=jnp.float32)
    damping = 1.0 / (1.0 + azimuth_damp * jnp.square(wavenum)[None, :] / jnp.square(radius)[:, None])
    slope_rate = jnp.where(wavenum < nyquist, wavenum * (2.0 * math.pi / NT), 0.0)
    courant = CZ * axial_rate
    factor = courant / (1.0 + courant)
    field_now = scalar
    for substep in range(SUBSTEPS):
        padded = jnp.pad(field_now, ((4, 4), (0, 0), (0, 0)))
        stencil_sum = jnp.zeros_like(field_now)
        for offset in range(9):
            stencil_sum = stencil_sum + stencil_coeffs[offset] * padded[offset:offset + NZ]
        explicit_field = field_now + axial_weight * stencil_sum
        solved = lax.linalg.tridiagonal_solve(sub_full, main_full, super_full, explicit_field)
        spectrum = jnp.fft.rfft(solved, axis=2) * damping
        smooth = jnp.fft.irfft(spectrum, n=NT, axis=2)
        azimuth_slope = jnp.fft.irfft(1j * slope_rate * spectrum, n=NT, axis=2)
        source = smooth - swirl_rate * azimuth_slope
        scaled = source / (1.0 + courant)

        def advance(carried, plane_pair):
            updated = plane_pair[0] * carried + plane_pair[1]
            return (updated, updated)
        final_value, field_now = lax.scan(advance, jnp.zeros((NR, NT), dtype=jnp.float32), (factor, scaled))
    return field_now
```

```python
import math

import jax
import jax.numpy as jnp
import ml_dtypes
import numpy as np
from jax import lax
from jax.sharding import PartitionSpec as P

CZ = 8
SUBSTEPS = 2
AXIAL_WEIGHT = 0.2
AZIMUTH_DAMP = 0.5
DIFFUSION = 1.0
STENCIL = (
    -1.0 / 560.0,
    8.0 / 315.0,
    -0.2,
    1.6,
    -205.0 / 72.0,
    1.6,
    -0.2,
    8.0 / 315.0,
    -1.0 / 560.0,
)
HALO = 4


def split_bf16(table):
    high = table.astype(ml_dtypes.bfloat16)
    low = (table - high.astype(np.float64)).astype(ml_dtypes.bfloat16)
    return high, low


def radial_tables(cells, groups):
    rows = cells // groups
    index = np.arange(cells, dtype=np.float64)
    radius = index + 0.5
    upper = np.where(index < cells - 1, index + 1.0, 0.0)
    sub = -DIFFUSION * index / radius
    sup = -DIFFUSION * upper / radius
    matrix = np.diag(1.0 - sub - sup) + np.diag(sub[1:], -1) + np.diag(sup[:-1], 1)
    green = np.linalg.inv(matrix)
    diag = np.diag(green)
    down = np.diag(green, -1) / diag[:-1]
    up = np.diag(green, 1) / diag[1:]
    local = np.zeros((groups, rows, rows))
    edges = np.zeros((groups, 2, rows))
    join = np.zeros((groups, rows, groups))
    for g in range(groups):
        first, last = g * rows, g * rows + rows - 1
        block = green[first : last + 1, first : last + 1]
        local[g] = block
        edges[g, 0] = block[-1]
        edges[g, 1] = block[0]
        for i in range(rows):
            for source in range(groups):
                if source < g:
                    join[g, i, source] = np.prod(down[source * rows + rows - 1 : first + i])
                elif source > g:
                    join[g, i, source] = np.prod(up[first + i : source * rows])
    return local, edges, join


def axial_tables(count, planes):
    table = np.zeros((count, planes, planes + 2 * HALO))
    for k in range(count):
        low, high = (0, planes + HALO) if k % 2 else (planes + HALO, 0)
        for plane in range(planes):
            for offset in range(-HALO, HALO + 1):
                value = AXIAL_WEIGHT * STENCIL[offset + HALO] + (1.0 if offset == 0 else 0.0)
                where = plane + offset
                if where < 0:
                    if k > 0:
                        table[k, plane, low + where + HALO] += value
                elif where >= planes:
                    if k < count - 1:
                        table[k, plane, high + where - planes] += value
                else:
                    table[k, plane, HALO + where] += value
    return table


def azimuth_tables(points):
    half = points // 2
    grid = np.arange(points)
    phase = (grid[:, None] * np.arange(half)[None, :]) % points
    angle = phase * (2.0 * math.pi / points)
    cosine, sine = np.cos(angle), np.sin(angle)
    sine[:, 0] = np.where(grid % 2 == 0, 1.0, -1.0)
    return np.concatenate([cosine, sine], axis=1)


def filter_tables(cells, points):
    half = points // 2
    radius = np.arange(cells) + 0.5
    wave = np.arange(half + 1.0)
    damp = 1.0 / (1.0 + AZIMUTH_DAMP * wave[None, :] ** 2 / radius[:, None] ** 2)
    weight = np.full(half + 1, 2.0 / points)
    weight[0] = weight[half] = 1.0 / points
    scaled = damp * weight
    rate = damp * (2.0 / points) * (wave * (2.0 * math.pi / points))
    smooth = np.concatenate([scaled[:, :half], scaled[:, half:], scaled[:, 1:half]], axis=1)
    slope = np.concatenate([rate[:, :half], -rate[:, :half]], axis=1)
    return smooth.astype(np.float32), slope.astype(np.float32)


def split_dot(values, high, low):
    coarse = lax.reduce_precision(values, 8, 7)
    fine = (values - coarse).astype(jnp.bfloat16)
    coarse = coarse.astype(jnp.bfloat16)
    out = jnp.dot(coarse, high, preferred_element_type=jnp.float32)
    out = out + jnp.dot(fine, high, preferred_element_type=jnp.float32)
    return out + jnp.dot(coarse, low, preferred_element_type=jnp.float32)


def exact_dot(matrix, values):
    return jnp.dot(
        matrix, values, precision=lax.Precision.HIGHEST, preferred_element_type=jnp.float32
    )


def swap(value, mask):
    count = lax.axis_size("ax")
    return lax.ppermute(value, "ax", [(i, i ^ mask) for i in range(count)])


def chain_swap(value):
    count = lax.axis_size("ax")
    pairs = [(i, (i + 1) % count if i % 2 else (i - 1) % count) for i in range(count)]
    return lax.ppermute(value, "ax", pairs)


def body(scalar, axial_rate, swirl_rate):
    planes, rows, points = scalar.shape
    half = points // 2
    groups = lax.axis_size("xs")
    count = lax.axis_size("ax")
    group = lax.axis_index("xs")
    place = lax.axis_index("ax")
    odd = place % 2 == 1
    upper = (place // 2) % 2 == 1
    quad = place // 4

    local, edges, join = radial_tables(rows * groups, groups)
    axial = axial_tables(count, planes)
    forward = azimuth_tables(points)
    fwd_high, fwd_low = split_bf16(forward)
    inv_high, inv_low = split_bf16(np.ascontiguousarray(forward.T))
    smooth_filter, slope_filter = filter_tables(rows * groups, points)

    def pick(table, index):
        return lax.dynamic_index_in_dim(jnp.asarray(table, jnp.float32), index, 0, keepdims=False)

    axial_here = pick(axial, place)
    local_here = pick(local, group)
    edges_here = pick(edges, group)
    join_here = pick(join, group)
    ext = planes + 2 * HALO
    solve_matrix = jnp.einsum("ze,ij->ziej", axial_here, local_here).reshape(
        planes * rows, ext * rows
    )
    edge_matrix = jnp.einsum("ze,sj->szej", axial_here, edges_here).reshape(
        2 * planes, ext * rows
    )
    join_matrix = jnp.einsum(
        "zy,is->zisy", jnp.eye(planes, dtype=jnp.float32), join_here
    ).reshape(planes * rows, groups * planes)
    smooth_here = lax.dynamic_slice_in_dim(jnp.asarray(smooth_filter), group * rows, rows, 0)
    slope_here = lax.dynamic_slice_in_dim(jnp.asarray(slope_filter), group * rows, rows, 0)

    courant = CZ * axial_rate
    inverse_rate = 1.0 / (1.0 + courant)
    factor = courant * inverse_rate
    swirl_scaled = swirl_rate * inverse_rate
    decays = [factor[0]]
    for plane in range(1, planes):
        decays.append(decays[-1] * factor[plane])
    decay = jnp.stack(decays)

    def pair_part(field):
        return jnp.where(odd, field[:HALO], field[planes - HALO :])

    def chain_part(field):
        return jnp.where(odd, field[planes - HALO :], field[:HALO])

    def own_half(value):
        return jnp.where(odd, value[:, half:], value[:, :half])

    def other_half(value):
        return jnp.where(odd, value[:, :half], value[:, half:])

    pair_field, chain_field = swap(pair_part(scalar), 1), chain_swap(chain_part(scalar))
    extended = jnp.concatenate([pair_field, scalar, chain_field], axis=0)
    pair_decay, chain_decay = swap(pair_part(decay), 1), chain_swap(chain_part(decay))
    pair_decay = jnp.where(odd, pair_decay / pair_decay[HALO - 1], pair_decay)
    chain_decay = jnp.where(odd, chain_decay, chain_decay / chain_decay[HALO - 1])

    field = scalar
    saved = None
    for substep in range(SUBSTEPS):
        flat = extended.reshape(ext * rows, points)
        carry = exact_dot(edge_matrix, flat).reshape(2, planes, points)
        ahead = (jnp.arange(groups) > group)[:, None, None]
        sent = jnp.where(ahead, carry[0][None], carry[1][None])
        got = lax.all_to_all(sent, "xs", split_axis=0, concat_axis=0, tiled=True)
        solved = exact_dot(solve_matrix, flat)
        solved = solved + exact_dot(join_matrix, got.reshape(groups * planes, points))
        spectrum = split_dot(solved, fwd_high, fwd_low).reshape(planes, rows, points)
        smooth_spec = spectrum * smooth_here
        slope_spec = (
            jnp.concatenate([spectrum[..., half:], spectrum[..., :half]], axis=-1) * slope_here
        )
        both = jnp.concatenate([smooth_spec, slope_spec], axis=0).reshape(-1, points)
        physical = split_dot(both, inv_high, inv_low).reshape(2, planes, rows, points)
        scaled = physical[0] * inverse_rate - swirl_scaled * physical[1]
        partials = [scaled[0]]
        for plane in range(1, planes):
            partials.append(factor[plane] * partials[-1] + scaled[plane])
        partial = jnp.stack(partials)
        last_step = substep == SUBSTEPS - 1
        if not last_step:
            pair_field, chain_field = swap(pair_part(partial), 1), chain_swap(chain_part(partial))

        total = partial[-1]
        if saved is None:
            span = decay[-1]
            got = swap(jnp.stack([other_half(total), other_half(span)]), 1)
            mine, span_mine = own_half(total), own_half(span)
            value0, value1 = jnp.where(odd, got[0], mine), jnp.where(odd, mine, got[0])
            span0, span1 = jnp.where(odd, got[1], span_mine), jnp.where(odd, span_mine, got[1])
            chip, chip_span = value1 + span1 * value0, span1 * span0
            got = swap(jnp.stack([chip, chip_span]), 2)
            behind_span = jnp.where(upper, got[1], 1.0)
            keep = jnp.where(upper, 1.0, got[1])
            take = jnp.where(upper, chip_span, 1.0)
            prefix = jnp.where(upper, got[0], 0.0)
            block = keep * chip + take * got[0]
            block_span = chip_span * got[1]
            pack = jnp.stack([block, block_span])
            got3, got2, got1 = swap(pack, 12), swap(pack, 8), swap(pack, 4)
            weight1 = jnp.where(quad % 2 == 1, behind_span, 0.0)
            weight2 = behind_span * jnp.where(
                quad == 2, got3[1], jnp.where(quad == 3, got1[1], 0.0)
            )
            weight3 = behind_span * jnp.where(
                quad == 2, 1.0, jnp.where(quad == 3, got1[1] * got2[1], 0.0)
            )
            got1, got2, got3 = got1[0], got2[0], got3[0]
            saved = (span0, span1, keep, take, weight1, weight2, weight3)
        else:
            span0, span1, keep, take, weight1, weight2, weight3 = saved
            got = swap(other_half(total), 1)
            mine = own_half(total)
            value0, value1 = jnp.where(odd, got, mine), jnp.where(odd, mine, got)
            chip = value1 + span1 * value0
            got = swap(chip, 2)
            prefix = jnp.where(upper, got, 0.0)
            block = keep * chip + take * got
            got3, got2, got1 = swap(block, 12), swap(block, 8), swap(block, 4)
        into0 = prefix + weight1 * got1 + weight2 * got2 + weight3 * got3
        into1 = span0 * into0 + value0
        mine, theirs = jnp.where(odd, into1, into0), jnp.where(odd, into0, into1)
        got = swap(theirs, 1)
        incoming = jnp.concatenate([jnp.where(odd, got, mine), jnp.where(odd, mine, got)], axis=1)
        field = partial + decay * incoming
        if not last_step:
            leaving = field[-1]
            pair_from = jnp.where(odd, incoming - pair_field[HALO - 1], leaving)
            chain_from = jnp.where(odd, leaving, incoming - chain_field[HALO - 1])
            extended = jnp.concatenate(
                [
                    pair_field + pair_decay * pair_from,
                    field,
                    chain_field + chain_decay * chain_from,
                ],
                axis=0,
            )
    return field


def solution(mesh):
    return jax.shard_map(
        body,
        mesh=mesh,
        in_specs=(P("ax", "xs", None), P("ax", "xs", None), P("ax", "xs", None)),
        out_specs=P("ax", "xs", None),
        check_vma=False,
    )
```

```python
import math

import jax
import jax.numpy as jnp
import ml_dtypes
import numpy as np
from jax import lax
from jax.experimental import pallas as pl
from jax.experimental.pallas import tpu as pltpu
from jax.sharding import PartitionSpec as P

CZ = 8
SUBSTEPS = 2
AXIAL_WEIGHT = 0.2
AZIMUTH_DAMP = 0.5
DIFFUSION = 1.0
STENCIL = (
    -1.0 / 560.0,
    8.0 / 315.0,
    -0.2,
    1.6,
    -205.0 / 72.0,
    1.6,
    -0.2,
    8.0 / 315.0,
    -1.0 / 560.0,
)
HALO = 4


def split_bf16(table):
    high = table.astype(ml_dtypes.bfloat16)
    low = (table - high.astype(np.float64)).astype(ml_dtypes.bfloat16)
    return high, low


def radial_tables(cells, groups, planes):
    rows = cells // groups
    index = np.arange(cells, dtype=np.float64)
    radius = index + 0.5
    upper = np.where(index < cells - 1, index + 1.0, 0.0)
    sub = -DIFFUSION * index / radius
    sup = -DIFFUSION * upper / radius
    matrix = np.diag(1.0 - sub - sup) + np.diag(sub[1:], -1) + np.diag(sup[:-1], 1)
    green = np.linalg.inv(matrix)
    diag = np.diag(green)
    down = np.diag(green, -1) / diag[:-1]
    up = np.diag(green, 1) / diag[1:]
    same = np.eye(planes)
    lines = planes * rows
    out = np.zeros((groups, lines + 2 * planes, lines + groups * planes), np.float32)
    for g in range(groups):
        first, last = g * rows, g * rows + rows - 1
        block = green[first : last + 1, first : last + 1]
        join = np.zeros((rows, groups))
        for i in range(rows):
            for source in range(groups):
                if source < g:
                    join[i, source] = np.prod(down[source * rows + rows - 1 : first + i])
                elif source > g:
                    join[i, source] = np.prod(up[first + i : source * rows])
        out[g, :lines, :lines] = np.kron(same, block)
        out[g, :lines, lines:] = np.einsum("zy,is->zisy", same, join).reshape(lines, -1)
        out[g, lines : lines + planes, :lines] = np.kron(same, block[-1:])
        out[g, lines + planes :, :lines] = np.kron(same, block[:1])
    return out


def azimuth_tables(points):
    half = points // 2
    quarter = half // 2
    grid = np.arange(half)
    out = []
    for parity in range(2):
        wave = 2 * np.arange(quarter) + parity
        angle = ((grid[:, None] * wave[None, :]) % points) * (2.0 * math.pi / points)
        cosine, sine = np.cos(angle), np.sin(angle)
        if parity == 0:
            sine[:, 0] = np.where(grid % 2 == 0, 1.0, -1.0)
        out.append(np.concatenate([cosine, sine], axis=1))
    return out


def filter_tables(cells, points):
    half = points // 2
    quarter = half // 2
    radius = np.arange(cells) + 0.5
    out = []
    for parity in range(2):
        wave = np.tile(2.0 * np.arange(quarter) + parity, 2)
        rate = wave * (2.0 * math.pi / points)
        weight = np.full(half, 2.0 / points)
        sign = np.repeat([1.0, -1.0], quarter)
        if parity == 0:
            wave[quarter] = half
            weight[0] = weight[quarter] = 1.0 / points
        damp = 1.0 / (1.0 + AZIMUTH_DAMP * wave[None, :] ** 2 / radius[:, None] ** 2)
        out.append((damp * weight, damp * (sign * rate * (2.0 / points))))
    table = [out[0][0], out[1][0], out[0][1], out[1][1]]
    return np.concatenate(table, axis=1).astype(np.float32)


def swap(value, mask):
    count = lax.axis_size("ax")
    return lax.ppermute(value, "ax", [(i, i ^ mask) for i in range(count)])


def chain_swap(value):
    count = lax.axis_size("ax")
    pairs = [(i, (i + 1) % count if i % 2 else (i - 1) % count) for i in range(count)]
    return lax.ppermute(value, "ax", pairs)


def split(values):
    coarse = values.astype(jnp.bfloat16)
    return coarse, (values - coarse.astype(jnp.float32)).astype(jnp.bfloat16)


def split_dot(left, right):
    dot = lambda x, y: jnp.dot(x, y, preferred_element_type=jnp.float32)
    return dot(left[0], right[0]) + (dot(left[1], right[0]) + dot(left[0], right[1]))


def carry_kernel(field, pair, chain, edges, explicit, sent):
    planes, rows, points = field.shape
    groups = sent.shape[0]
    place = lax.axis_index("ax")
    group = lax.axis_index("xs")
    odd = place % 2 == 1
    low_scale = jnp.where(place > 0, 1.0, 0.0)
    high_scale = jnp.where(place < lax.axis_size("ax") - 1, 1.0, 0.0)
    quarter = points // 4
    for part in range(4):
        where = slice(part * quarter, (part + 1) * quarter)
        low = [jnp.where(odd, pair[j, :, where], chain[j, :, where]) for j in range(HALO)]
        high = [jnp.where(odd, chain[j, :, where], pair[j, :, where]) for j in range(HALO)]
        every = [low_scale * value for value in low]
        every += [field[plane, :, where] for plane in range(planes)]
        every += [high_scale * value for value in high]
        for plane in range(planes):
            value = (1.0 + AXIAL_WEIGHT * STENCIL[HALO]) * every[plane + HALO]
            for step in range(1, HALO + 1):
                both = every[plane + HALO - step] + every[plane + HALO + step]
                value = value + (AXIAL_WEIGHT * STENCIL[HALO + step]) * both
            explicit[plane, :, where] = value
    lines = explicit[...].reshape(planes * rows, points)
    carry = split_dot(split(edges[...]), split(lines))
    for target in range(groups):
        sent[target] = jnp.where(target > group, carry[:planes], carry[planes:])


def middle_kernel(
    explicit,
    got,
    matrix,
    forward,
    inverse,
    filters,
    axial_rate,
    swirl_rate,
    partial,
    decay,
    mine,
    other,
):
    planes, rows, points = partial.shape
    half = points // 2
    quarter = half // 2
    lines = planes * rows
    known = jnp.concatenate([explicit[...].reshape(lines, points), got[...]], axis=0)
    solved = split_dot(split(matrix[...]), split(known))
    sides = (solved[:, :half] + solved[:, half:], solved[:, :half] - solved[:, half:])
    periods = []
    for parity in range(2):
        table = (forward[parity, 0], forward[parity, 1])
        spectrum = split_dot(split(sides[parity]), table).reshape(planes, rows, half)
        swapped = jnp.concatenate([spectrum[..., quarter:], spectrum[..., :quarter]], axis=-1)
        smooth = spectrum * filters[:, parity * half : (parity + 1) * half]
        slope = swapped * filters[:, points + parity * half : points + (parity + 1) * half]
        both = jnp.concatenate([smooth, slope], axis=0).reshape(2 * planes * rows, half)
        table = (inverse[parity, 0], inverse[parity, 1])
        periods.append(split_dot(split(both), table).reshape(2, planes, rows, half))
    for side in range(2):
        where = slice(side * half, (side + 1) * half)
        value = fade = None
        for plane in range(planes):
            even, odd = periods[0][:, plane], periods[1][:, plane]
            both = even + odd if side == 0 else even - odd
            courant = CZ * axial_rate[plane, :, where]
            inverse_rate = 1.0 / (1.0 + courant)
            factor = courant * inverse_rate
            scaled = inverse_rate * (both[0] - swirl_rate[plane, :, where] * both[1])
            value = scaled if plane == 0 else factor * value + scaled
            fade = factor if plane == 0 else factor * fade
            partial[plane, :, where] = value
            decay[plane, :, where] = fade
        is_mine = lax.axis_index("ax") % 2 == side
        for index, last in enumerate((value, fade)[: mine.shape[0]]):

            @pl.when(is_mine)
            def _():
                mine[index] = last

            @pl.when(jnp.logical_not(is_mine))
            def _():
                other[index] = last


def ends_kernel(field, pair, chain):
    planes = field.shape[0]
    odd = lax.axis_index("ax") % 2 == 1
    for j in range(HALO):
        low, high = field[j], field[planes - HALO + j]
        pair[j] = jnp.where(odd, low, high)
        chain[j] = jnp.where(odd, high, low)


def chip_kernel(mine, got, *refs):
    odd = lax.axis_index("ax") % 2 == 1
    value0, value1 = jnp.where(odd, got[0], mine[0]), jnp.where(odd, mine[0], got[0])
    if mine.shape[0] == 2:
        block, behind, spans = refs
        span0, span1 = jnp.where(odd, got[1], mine[1]), jnp.where(odd, mine[1], got[1])
        block[1] = span0 * span1
        spans[0], spans[1] = span0, span1
    else:
        spans, block, behind = refs
        span1 = spans[1]
    block[0] = value1 + span1 * value0
    behind[...] = value0


def couple_kernel(block, got, *refs):
    upper = (lax.axis_index("ax") // 2) % 2 == 1
    if block.shape[0] == 2:
        joint, prefix, gains = refs
        joint[1] = block[1] * got[1]
        gains[0] = jnp.where(upper, 1.0, got[1])
        gains[1] = jnp.where(upper, block[1], 1.0)
        gains[2] = jnp.where(upper, got[1], 1.0)
    else:
        gains, joint, prefix = refs
    joint[0] = gains[0] * block[0] + gains[1] * got[0]
    prefix[...] = jnp.where(upper, got[0], 0.0)


def enter_kernel(got1, got2, got3, prefix, behind, spans, gains, *refs):
    place = lax.axis_index("ax")
    odd = place % 2 == 1
    quad = place // 4
    if got1.shape[0] == 2:
        mine, other, weights = refs
        before = gains[2]
        weights[0] = jnp.where(quad % 2 == 1, before, 0.0)
        weights[1] = before * jnp.where(quad == 2, got3[1], jnp.where(quad == 3, got1[1], 0.0))
        weights[2] = before * jnp.where(
            quad == 2, 1.0, jnp.where(quad == 3, got1[1] * got2[1], 0.0)
        )
    else:
        weights, mine, other = refs
    into0 = prefix[...] + weights[0] * got1[0] + weights[1] * got2[0] + weights[2] * got3[0]
    into1 = spans[0] * into0 + behind[...]
    mine[...] = jnp.where(odd, into1, into0)
    other[...] = jnp.where(odd, into0, into1)


def finish_kernel(partial, decay, mine, got, field, pair, chain):
    planes, rows, points = partial.shape
    half = points // 2
    odd = lax.axis_index("ax") % 2 == 1
    for side in range(2):
        where = slice(side * half, (side + 1) * half)
        incoming = jnp.where(odd == (side == 1), mine[...], got[...])
        ends = {}
        for plane in range(planes):
            value = partial[plane, :, where] + decay[plane, :, where] * incoming
            field[plane, :, where] = value
            ends[plane] = value
        for j in range(HALO):
            low, high = ends[j], ends[planes - HALO + j]
            pair[j, :, where] = jnp.where(odd, low, high)
            chain[j, :, where] = jnp.where(odd, high, low)


def call(kernel, out_shape, *args, vmem=4):
    return pl.pallas_call(
        kernel,
        out_shape=out_shape,
        in_specs=[pl.BlockSpec(memory_space=pltpu.VMEM)] * len(args),
        out_specs=jax.tree.map(lambda _: pl.BlockSpec(memory_space=pltpu.VMEM), out_shape),
        compiler_params=pltpu.CompilerParams(vmem_limit_bytes=vmem * 1024 * 1024),
    )(*args)


def body(scalar, axial_rate, swirl_rate):
    planes, rows, points = scalar.shape
    half = points // 2
    groups = lax.axis_size("xs")
    group = lax.axis_index("xs")
    place = lax.axis_index("ax")
    odd = place % 2 == 1
    lines = planes * rows
    tables = azimuth_tables(points)
    forward = jnp.asarray(np.stack([np.stack(split_bf16(t)) for t in tables]))
    inverse = jnp.asarray(np.stack([np.stack(split_bf16(t.T)) for t in tables]))
    radial = lax.dynamic_index_in_dim(
        jnp.asarray(radial_tables(rows * groups, groups, planes)), group, 0, keepdims=False
    )
    matrix, edges = radial[:lines], radial[lines:, :lines]
    filters = lax.dynamic_slice_in_dim(
        jnp.asarray(filter_tables(rows * groups, points)), group * rows, rows, 0
    )
    block = jax.ShapeDtypeStruct((planes, rows, points), jnp.float32)

    ends = jax.ShapeDtypeStruct((HALO, rows, points), jnp.float32)

    def halves(count):
        return jax.ShapeDtypeStruct((count, rows, half), jnp.float32)

    plane_half = jax.ShapeDtypeStruct((rows, half), jnp.float32)

    field = scalar
    pair_end, chain_end = call(ends_kernel, (ends, ends), scalar)
    saved = None
    for substep in range(SUBSTEPS):
        chain, pair = chain_swap(chain_end), swap(pair_end, 1)
        explicit, sent = call(
            carry_kernel,
            (block, jax.ShapeDtypeStruct((groups, planes, points), jnp.float32)),
            field,
            pair,
            chain,
            edges,
        )
        got = lax.all_to_all(sent, "xs", split_axis=0, concat_axis=0, tiled=True)
        first = saved is None
        parts = 2 if first else 1
        partial, decay, mine, other = call(
            middle_kernel,
            (block, block, halves(parts), halves(parts)),
            explicit,
            got.reshape(groups * planes, points),
            matrix,
            forward,
            inverse,
            filters,
            axial_rate,
            swirl_rate,
            vmem=16,
        )
        got = swap(other, 1)
        if first:
            value, behind, spans = call(
                chip_kernel, (halves(2), plane_half, halves(2)), mine, got
            )
        else:
            value, behind = call(chip_kernel, (halves(1), plane_half), mine, got, spans)
        got = swap(value, 2)
        if first:
            value, prefix, gains = call(
                couple_kernel, (halves(2), plane_half, halves(3)), value, got
            )
        else:
            value, prefix = call(couple_kernel, (halves(1), plane_half), value, got, gains)
        got3, got2, got1 = swap(value, 12), swap(value, 8), swap(value, 4)
        args = (got1, got2, got3, prefix, behind, spans, gains)
        if first:
            mine, other, saved = call(enter_kernel, (plane_half, plane_half, halves(3)), *args)
        else:
            mine, other = call(enter_kernel, (plane_half, plane_half), *args, saved)
        got = swap(other, 1)
        if substep < SUBSTEPS - 1:
            field, pair_end, chain_end = call(
                finish_kernel, (block, ends, ends), partial, decay, mine, got
            )
        else:
            incoming = jnp.concatenate(
                [jnp.where(odd, got, mine), jnp.where(odd, mine, got)], axis=1
            )
            field = partial + decay * incoming
    return field


def solution(mesh):
    return jax.shard_map(
        body,
        mesh=mesh,
        in_specs=(P("ax", "xs", None), P("ax", "xs", None), P("ax", "xs", None)),
        out_specs=P("ax", "xs", None),
        check_vma=False,
    )
```

```python
import math

import jax
import jax.numpy as jnp
import ml_dtypes
import numpy as np
from jax import lax
from jax.experimental import pallas as pl
from jax.experimental.pallas import tpu as pltpu
from jax.sharding import PartitionSpec as P

CZ = 8
SUBSTEPS = 2
AXIAL_WEIGHT = 0.2
AZIMUTH_DAMP = 0.5
DIFFUSION = 1.0
STENCIL = (
    -1.0 / 560.0,
    8.0 / 315.0,
    -0.2,
    1.6,
    -205.0 / 72.0,
    1.6,
    -0.2,
    8.0 / 315.0,
    -1.0 / 560.0,
)
HALO = 4


def split_bf16(table):
    high = table.astype(ml_dtypes.bfloat16)
    low = (table - high.astype(np.float64)).astype(ml_dtypes.bfloat16)
    return high, low


def radial_tables(cells, groups, planes):
    rows = cells // groups
    index = np.arange(cells, dtype=np.float64)
    radius = index + 0.5
    upper = np.where(index < cells - 1, index + 1.0, 0.0)
    sub = -DIFFUSION * index / radius
    sup = -DIFFUSION * upper / radius
    matrix = np.diag(1.0 - sub - sup) + np.diag(sub[1:], -1) + np.diag(sup[:-1], 1)
    green = np.linalg.inv(matrix)
    diag = np.diag(green)
    down = np.diag(green, -1) / diag[:-1]
    up = np.diag(green, 1) / diag[1:]
    same = np.eye(planes)
    lines = planes * rows
    out = np.zeros((groups, lines + 2 * planes, lines + groups * planes), np.float32)
    for g in range(groups):
        first, last = g * rows, g * rows + rows - 1
        block = green[first : last + 1, first : last + 1]
        join = np.zeros((rows, groups))
        for i in range(rows):
            for source in range(groups):
                if source < g:
                    join[i, source] = np.prod(down[source * rows + rows - 1 : first + i])
                elif source > g:
                    join[i, source] = np.prod(up[first + i : source * rows])
        out[g, :lines, :lines] = np.kron(same, block)
        out[g, :lines, lines:] = np.einsum("zy,is->zisy", same, join).reshape(lines, -1)
        out[g, lines : lines + planes, :lines] = np.kron(same, block[-1:])
        out[g, lines + planes :, :lines] = np.kron(same, block[:1])
    return out


def azimuth_tables(points):
    half = points // 2
    quarter = half // 2
    grid = np.arange(half)
    out = []
    for parity in range(2):
        wave = 2 * np.arange(quarter) + parity
        angle = ((grid[:, None] * wave[None, :]) % points) * (2.0 * math.pi / points)
        cosine, sine = np.cos(angle), np.sin(angle)
        if parity == 0:
            sine[:, 0] = np.where(grid % 2 == 0, 1.0, -1.0)
        out.append(np.concatenate([cosine, sine], axis=1))
    return out


def filter_tables(cells, points):
    half = points // 2
    quarter = half // 2
    radius = np.arange(cells) + 0.5
    out = []
    for parity in range(2):
        wave = np.tile(2.0 * np.arange(quarter) + parity, 2)
        rate = wave * (2.0 * math.pi / points)
        weight = np.full(half, 2.0 / points)
        sign = np.repeat([1.0, -1.0], quarter)
        if parity == 0:
            wave[quarter] = half
            weight[0] = weight[quarter] = 1.0 / points
        damp = 1.0 / (1.0 + AZIMUTH_DAMP * wave[None, :] ** 2 / radius[:, None] ** 2)
        out.append((damp * weight, damp * (sign * rate * (2.0 / points))))
    table = [out[0][0], out[1][0], out[0][1], out[1][1]]
    return np.concatenate(table, axis=1).astype(np.float32)


def swap(value, mask):
    count = lax.axis_size("ax")
    return lax.ppermute(value, "ax", [(i, i ^ mask) for i in range(count)])


def chain_swap(value):
    count = lax.axis_size("ax")
    pairs = [(i, (i + 1) % count if i % 2 else (i - 1) % count) for i in range(count)]
    return lax.ppermute(value, "ax", pairs)


def split(values):
    coarse = values.astype(jnp.bfloat16)
    return coarse, (values - coarse.astype(jnp.float32)).astype(jnp.bfloat16)


def split_dot(left, right, depth=0):
    def dot(x, y):
        return lax.dot_general(
            x, y, (((1,), (depth,)), ((), ())), preferred_element_type=jnp.float32
        )

    return dot(left[0], right[0]) + (dot(left[1], right[0]) + dot(left[0], right[1]))


def setup_kernel(radial, damping, matrix, edges, filters, sems):
    group = lax.axis_index("xs")
    lines, columns = matrix.shape[0], edges.shape[1]
    copies = [
        pltpu.make_async_copy(
            radial.at[group, pl.ds(lines, edges.shape[0]), pl.ds(0, columns)], edges, sems.at[0]
        ),
        pltpu.make_async_copy(radial.at[group, pl.ds(0, lines)], matrix, sems.at[1]),
        pltpu.make_async_copy(damping.at[group], filters, sems.at[2]),
    ]
    for copy in copies:
        copy.start()
    for copy in copies:
        copy.wait()


def inner_kernel(field, inner):
    planes = field.shape[0]
    for plane in range(planes):
        value = (1.0 + AXIAL_WEIGHT * STENCIL[HALO]) * field[plane]
        for source in range(max(0, plane - HALO), min(planes, plane + HALO + 1)):
            if source != plane:
                value = value + (AXIAL_WEIGHT * STENCIL[HALO + source - plane]) * field[source]
        inner[plane] = value


def carry_kernel(inner, pair, chain, edges, explicit, sent):
    planes, rows, points = inner.shape
    groups = sent.shape[0]
    place = lax.axis_index("ax")
    group = lax.axis_index("xs")
    odd = place % 2 == 1
    low_scale = jnp.where(place > 0, 1.0, 0.0)
    high_scale = jnp.where(place < lax.axis_size("ax") - 1, 1.0, 0.0)
    quarter = points // 4
    for part in range(4):
        where = slice(part * quarter, (part + 1) * quarter)
        low = [jnp.where(odd, pair[j, :, where], chain[j, :, where]) for j in range(HALO)]
        high = [jnp.where(odd, chain[j, :, where], pair[j, :, where]) for j in range(HALO)]
        low = [low_scale * value for value in low]
        high = [high_scale * value for value in high]
        for plane in range(planes):
            value = inner[plane, :, where]
            for j in range(HALO):
                if plane + HALO - j <= HALO:
                    value = value + (AXIAL_WEIGHT * STENCIL[j - plane]) * low[j]
                if planes + j - plane <= HALO:
                    value = value + (AXIAL_WEIGHT * STENCIL[HALO + planes + j - plane]) * high[j]
            explicit[plane, :, where] = value
    lines = explicit[...].reshape(planes * rows, points)
    carry = split_dot(split(edges[...]), split(lines))
    for target in range(groups):
        sent[target] = jnp.where(target > group, carry[:planes], carry[planes:])


def middle_kernel(
    explicit,
    got,
    matrix,
    azimuth,
    filters,
    axial_rate,
    swirl_rate,
    partial,
    decay,
    mine,
    other,
):
    planes, rows, points = partial.shape
    half = points // 2
    quarter = half // 2
    lines = planes * rows
    known = jnp.concatenate([explicit[...].reshape(lines, points), got[...]], axis=0)
    solved = split_dot(split(matrix[...]), split(known))
    sides = (solved[:, :half] + solved[:, half:], solved[:, :half] - solved[:, half:])
    periods = []
    for parity in range(2):
        table = (azimuth[parity, 0], azimuth[parity, 1])
        spectrum = split_dot(split(sides[parity]), table).reshape(planes, rows, half)
        swapped = jnp.concatenate([spectrum[..., quarter:], spectrum[..., :quarter]], axis=-1)
        smooth = spectrum * filters[:, parity * half : (parity + 1) * half]
        slope = swapped * filters[:, points + parity * half : points + (parity + 1) * half]
        both = jnp.concatenate([smooth, slope], axis=0).reshape(2 * planes * rows, half)
        periods.append(split_dot(split(both), table, 1).reshape(2, planes, rows, half))
    for side in range(2):
        where = slice(side * half, (side + 1) * half)
        value = fade = None
        for plane in range(planes):
            even, odd = periods[0][:, plane], periods[1][:, plane]
            both = even + odd if side == 0 else even - odd
            courant = CZ * axial_rate[plane, :, where]
            inverse_rate = 1.0 / (1.0 + courant)
            factor = courant * inverse_rate
            scaled = inverse_rate * (both[0] - swirl_rate[plane, :, where] * both[1])
            value = scaled if plane == 0 else factor * value + scaled
            fade = factor if plane == 0 else factor * fade
            partial[plane, :, where] = value
            decay[plane, :, where] = fade
        is_mine = lax.axis_index("ax") % 2 == side
        for index, last in enumerate((value, fade)[: mine.shape[0]]):

            @pl.when(is_mine)
            def _():
                mine[index] = last

            @pl.when(jnp.logical_not(is_mine))
            def _():
                other[index] = last


def ends_kernel(field, pair, chain):
    planes = field.shape[0]
    odd = lax.axis_index("ax") % 2 == 1
    for j in range(HALO):
        low, high = field[j], field[planes - HALO + j]
        pair[j] = jnp.where(odd, low, high)
        chain[j] = jnp.where(odd, high, low)


def chip_kernel(mine, got, *refs):
    odd = lax.axis_index("ax") % 2 == 1
    value0, value1 = jnp.where(odd, got[0], mine[0]), jnp.where(odd, mine[0], got[0])
    if mine.shape[0] == 2:
        block, behind, spans = refs
        span0, span1 = jnp.where(odd, got[1], mine[1]), jnp.where(odd, mine[1], got[1])
        block[1] = span0 * span1
        spans[0], spans[1] = span0, span1
    else:
        spans, block, behind = refs
        span1 = spans[1]
    block[0] = value1 + span1 * value0
    behind[...] = value0


def couple_kernel(block, got, *refs):
    upper = (lax.axis_index("ax") // 2) % 2 == 1
    if block.shape[0] == 2:
        joint, prefix, gains = refs
        joint[1] = block[1] * got[1]
        gains[0] = jnp.where(upper, 1.0, got[1])
        gains[1] = jnp.where(upper, block[1], 1.0)
        gains[2] = jnp.where(upper, got[1], 1.0)
    else:
        gains, joint, prefix = refs
    joint[0] = gains[0] * block[0] + gains[1] * got[0]
    prefix[...] = jnp.where(upper, got[0], 0.0)


def enter_kernel(got1, got2, got3, prefix, behind, spans, gains, *refs):
    place = lax.axis_index("ax")
    odd = place % 2 == 1
    quad = place // 4
    if got1.shape[0] == 2:
        mine, other, weights = refs
        before = gains[2]
        weights[0] = jnp.where(quad % 2 == 1, before, 0.0)
        weights[1] = before * jnp.where(quad == 2, got3[1], jnp.where(quad == 3, got1[1], 0.0))
        weights[2] = before * jnp.where(
            quad == 2, 1.0, jnp.where(quad == 3, got1[1] * got2[1], 0.0)
        )
    else:
        weights, mine, other = refs
    into0 = prefix[...] + weights[0] * got1[0] + weights[1] * got2[0] + weights[2] * got3[0]
    into1 = spans[0] * into0 + behind[...]
    mine[...] = jnp.where(odd, into1, into0)
    other[...] = jnp.where(odd, into0, into1)


def finish_kernel(partial, decay, mine, got, field, pair, chain):
    planes, rows, points = partial.shape
    half = points // 2
    odd = lax.axis_index("ax") % 2 == 1
    for side in range(2):
        where = slice(side * half, (side + 1) * half)
        incoming = jnp.where(odd == (side == 1), mine[...], got[...])
        ends = {}
        for plane in range(planes):
            value = partial[plane, :, where] + decay[plane, :, where] * incoming
            field[plane, :, where] = value
            ends[plane] = value
        for j in range(HALO):
            low, high = ends[j], ends[planes - HALO + j]
            pair[j, :, where] = jnp.where(odd, low, high)
            chain[j, :, where] = jnp.where(odd, high, low)


def last_kernel(partial, decay, mine, got, out, field, sems):
    planes, rows, points = partial.shape
    half = points // 2
    odd = lax.axis_index("ax") % 2 == 1
    incoming = [jnp.where(odd == (side == 1), mine[...], got[...]) for side in range(2)]
    copies = []
    for plane in range(planes):
        for side in range(2):
            where = slice(side * half, (side + 1) * half)
            value = partial[plane, :, where] + decay[plane, :, where] * incoming[side]
            field[plane, :, where] = value
        if plane % 2 == 1:
            pair = pl.ds(plane - 1, 2)
            copy = pltpu.make_async_copy(field.at[pair], out.at[pair], sems.at[plane // 2])
            copy.start()
            copies.append(copy)
    for copy in copies:
        copy.wait()


def call(kernel, out_shape, *args, vmem=4):
    return pl.pallas_call(
        kernel,
        out_shape=out_shape,
        in_specs=[pl.BlockSpec(memory_space=pltpu.VMEM)] * len(args),
        out_specs=jax.tree.map(lambda _: pl.BlockSpec(memory_space=pltpu.VMEM), out_shape),
        compiler_params=pltpu.CompilerParams(vmem_limit_bytes=vmem * 1024 * 1024),
    )(*args)


def body(scalar, axial_rate, swirl_rate):
    planes, rows, points = scalar.shape
    half = points // 2
    groups = lax.axis_size("xs")
    lines = planes * rows
    tables = azimuth_tables(points)
    azimuth = jnp.asarray(np.stack([np.stack(split_bf16(t)) for t in tables]))
    radial = radial_tables(rows * groups, groups, planes)
    damping = filter_tables(rows * groups, points).reshape(groups, rows, 2 * points)

    def shape(*sizes):
        return jax.ShapeDtypeStruct(sizes, jnp.float32)

    block, ends, one = shape(planes, rows, points), shape(HALO, rows, points), shape(rows, half)

    pair_end, chain_end = call(ends_kernel, (ends, ends), scalar)
    chain, pair = chain_swap(chain_end), swap(pair_end, 1)
    inner = call(inner_kernel, block, scalar)
    matrix, edges, filters = pl.pallas_call(
        setup_kernel,
        out_shape=(
            shape(lines, lines + groups * planes),
            shape(2 * planes, lines),
            shape(rows, 2 * points),
        ),
        in_specs=[pl.BlockSpec(memory_space=pltpu.HBM)] * 2,
        out_specs=(pl.BlockSpec(memory_space=pltpu.VMEM),) * 3,
        scratch_shapes=[pltpu.SemaphoreType.DMA((3,))],
        compiler_params=pltpu.CompilerParams(vmem_limit_bytes=4 * 1024 * 1024),
    )(jnp.asarray(radial), jnp.asarray(damping))

    for substep in range(SUBSTEPS):
        explicit, sent = call(
            carry_kernel, (block, shape(groups, planes, points)), inner, pair, chain, edges
        )
        got = lax.all_to_all(sent, "xs", split_axis=0, concat_axis=0, tiled=True)
        first = substep == 0
        parts = shape(2 if first else 1, rows, half)
        partial, decay, mine, other = call(
            middle_kernel,
            (block, block, parts, parts),
            explicit,
            got.reshape(groups * planes, points),
            matrix,
            azimuth,
            filters,
            axial_rate,
            swirl_rate,
            vmem=16,
        )
        got = swap(other, 1)
        if first:
            value, behind, spans = call(chip_kernel, (parts, one, parts), mine, got)
        else:
            value, behind = call(chip_kernel, (parts, one), mine, got, spans)
        got = swap(value, 2)
        if first:
            out = (parts, one, shape(3, rows, half))
            value, prefix, gains = call(couple_kernel, out, value, got)
        else:
            value, prefix = call(couple_kernel, (parts, one), value, got, gains)
        far3, far2, far1 = swap(value, 12), swap(value, 8), swap(value, 4)
        args = (far1, far2, far3, prefix, behind, spans, gains)
        if first:
            mine, other, weights = call(enter_kernel, (one, one, shape(3, rows, half)), *args)
        else:
            mine, other = call(enter_kernel, (one, one), *args, weights)
        got = swap(other, 1)
        if substep < SUBSTEPS - 1:
            field, pair_end, chain_end = call(
                finish_kernel, (block, ends, ends), partial, decay, mine, got
            )
            chain, pair = chain_swap(chain_end), swap(pair_end, 1)
            inner = call(inner_kernel, block, field)
    return pl.pallas_call(
        last_kernel,
        out_shape=block,
        in_specs=[pl.BlockSpec(memory_space=pltpu.VMEM)] * 4,
        out_specs=pl.BlockSpec(memory_space=pl.ANY),
        scratch_shapes=[
            pltpu.VMEM((planes, rows, points), jnp.float32),
            pltpu.SemaphoreType.DMA((planes // 2,)),
        ],
        compiler_params=pltpu.CompilerParams(vmem_limit_bytes=4 * 1024 * 1024),
    )(partial, decay, mine, got)


def solution(mesh):
    return jax.shard_map(
        body,
        mesh=mesh,
        in_specs=(P("ax", "xs", None), P("ax", "xs", None), P("ax", "xs", None)),
        out_specs=P("ax", "xs", None),
        check_vma=False,
    )
```

```python
import math

import jax
import jax.numpy as jnp
import ml_dtypes
import numpy as np
from jax import lax
from jax.experimental import pallas as pl
from jax.experimental.pallas import tpu as pltpu
from jax.sharding import PartitionSpec as P

CZ = 8
SUBSTEPS = 2
AXIAL_WEIGHT = 0.2
AZIMUTH_DAMP = 0.5
DIFFUSION = 1.0
STENCIL = (
    -1.0 / 560.0,
    8.0 / 315.0,
    -0.2,
    1.6,
    -205.0 / 72.0,
    1.6,
    -0.2,
    8.0 / 315.0,
    -1.0 / 560.0,
)
HALO = 4
FAR = ((7, 1), (3, 7), (5, 2), (4, 6))


def split_bf16(table):
    high = table.astype(ml_dtypes.bfloat16)
    low = (table - high.astype(np.float64)).astype(ml_dtypes.bfloat16)
    return high, low


def radial_tables(cells, groups, planes):
    rows = cells // groups
    index = np.arange(cells, dtype=np.float64)
    radius = index + 0.5
    upper = np.where(index < cells - 1, index + 1.0, 0.0)
    sub = -DIFFUSION * index / radius
    sup = -DIFFUSION * upper / radius
    matrix = np.diag(1.0 - sub - sup) + np.diag(sub[1:], -1) + np.diag(sup[:-1], 1)
    green = np.linalg.inv(matrix)
    diag = np.diag(green)
    down = np.diag(green, -1) / diag[:-1]
    up = np.diag(green, 1) / diag[1:]
    same = np.eye(planes)
    lines = planes * rows
    out = np.zeros((groups, lines + 2 * planes, lines + groups * planes), np.float32)
    for g in range(groups):
        first, last = g * rows, g * rows + rows - 1
        block = green[first : last + 1, first : last + 1]
        join = np.zeros((rows, groups))
        for i in range(rows):
            for source in range(groups):
                if source < g:
                    join[i, source] = np.prod(down[source * rows + rows - 1 : first + i])
                elif source > g:
                    join[i, source] = np.prod(up[first + i : source * rows])
        out[g, :lines, :lines] = np.kron(same, block)
        out[g, :lines, lines:] = np.einsum("zy,is->zisy", same, join).reshape(lines, -1)
        out[g, lines : lines + planes, :lines] = np.kron(same, block[-1:])
        out[g, lines + planes :, :lines] = np.kron(same, block[:1])
    return out


def azimuth_tables(points):
    half = points // 2
    quarter = half // 2
    grid = np.arange(half)
    out = []
    for parity in range(2):
        wave = 2 * np.arange(quarter) + parity
        angle = ((grid[:, None] * wave[None, :]) % points) * (2.0 * math.pi / points)
        cosine, sine = np.cos(angle), np.sin(angle)
        if parity == 0:
            sine[:, 0] = np.where(grid % 2 == 0, 1.0, -1.0)
        out.append(np.concatenate([cosine, sine], axis=1))
    return out


def filter_tables(cells, points):
    half = points // 2
    quarter = half // 2
    radius = np.arange(cells) + 0.5
    out = []
    for parity in range(2):
        wave = np.tile(2.0 * np.arange(quarter) + parity, 2)
        rate = wave * (2.0 * math.pi / points)
        weight = np.full(half, 2.0 / points)
        sign = np.repeat([1.0, -1.0], quarter)
        if parity == 0:
            wave[quarter] = half
            weight[0] = weight[quarter] = 1.0 / points
        damp = 1.0 / (1.0 + AZIMUTH_DAMP * wave[None, :] ** 2 / radius[:, None] ** 2)
        out.append((damp * weight, damp * (sign * rate * (2.0 / points))))
    table = [out[0][0], out[1][0], out[0][1], out[1][1]]
    return np.concatenate(table, axis=1).astype(np.float32)


def swap(value, mask):
    count = lax.axis_size("ax")
    return lax.ppermute(value, "ax", [(i, i ^ mask) for i in range(count)])


def far_swap(value, masks):
    count = lax.axis_size("ax")
    return lax.ppermute(value, "ax", [(i, i ^ 2 * masks[1 - i % 2]) for i in range(count)])


def chain_swap(value):
    count = lax.axis_size("ax")
    pairs = [(i, (i + 1) % count if i % 2 else (i - 1) % count) for i in range(count)]
    return lax.ppermute(value, "ax", pairs)


def split(values):
    coarse = values.astype(jnp.bfloat16)
    return coarse, (values - coarse.astype(jnp.float32)).astype(jnp.bfloat16)


def split_dot(left, right, depth=0):
    def dot(x, y):
        return lax.dot_general(
            x, y, (((1,), (depth,)), ((), ())), preferred_element_type=jnp.float32
        )

    return dot(left[0], right[0]) + (dot(left[1], right[0]) + dot(left[0], right[1]))


def setup_kernel(radial, damping, matrix, edges, filters, sems):
    group = lax.axis_index("xs")
    lines, columns = matrix.shape[0], edges.shape[1]
    copies = [
        pltpu.make_async_copy(
            radial.at[group, pl.ds(lines, edges.shape[0]), pl.ds(0, columns)], edges, sems.at[0]
        ),
        pltpu.make_async_copy(radial.at[group, pl.ds(0, lines)], matrix, sems.at[1]),
        pltpu.make_async_copy(damping.at[group], filters, sems.at[2]),
    ]
    for copy in copies:
        copy.start()
    for copy in copies:
        copy.wait()


def inner_kernel(field, inner):
    planes = field.shape[0]
    for plane in range(planes):
        value = (1.0 + AXIAL_WEIGHT * STENCIL[HALO]) * field[plane]
        for source in range(max(0, plane - HALO), min(planes, plane + HALO + 1)):
            if source != plane:
                value = value + (AXIAL_WEIGHT * STENCIL[HALO + source - plane]) * field[source]
        inner[plane] = value


def carry_kernel(inner, pair, chain, edges, explicit, sent):
    planes, rows, points = inner.shape
    groups = sent.shape[0]
    place = lax.axis_index("ax")
    group = lax.axis_index("xs")
    odd = place % 2 == 1
    low_scale = jnp.where(place > 0, 1.0, 0.0)
    high_scale = jnp.where(place < lax.axis_size("ax") - 1, 1.0, 0.0)
    quarter = points // 4
    for part in range(4):
        where = slice(part * quarter, (part + 1) * quarter)
        low = [jnp.where(odd, pair[j, :, where], chain[j, :, where]) for j in range(HALO)]
        high = [jnp.where(odd, chain[j, :, where], pair[j, :, where]) for j in range(HALO)]
        low = [low_scale * value for value in low]
        high = [high_scale * value for value in high]
        for plane in range(planes):
            value = inner[plane, :, where]
            for j in range(HALO):
                if plane + HALO - j <= HALO:
                    value = value + (AXIAL_WEIGHT * STENCIL[j - plane]) * low[j]
                if planes + j - plane <= HALO:
                    value = value + (AXIAL_WEIGHT * STENCIL[HALO + planes + j - plane]) * high[j]
            explicit[plane, :, where] = value
    lines = explicit[...].reshape(planes * rows, points)
    carry = split_dot(split(edges[...]), split(lines))
    for target in range(groups):
        sent[target] = jnp.where(target > group, carry[:planes], carry[planes:])


def middle_kernel(
    explicit,
    got,
    matrix,
    azimuth,
    filters,
    axial_rate,
    swirl_rate,
    partial,
    decay,
    mine,
    other=None,
):
    planes, rows, points = partial.shape
    half = points // 2
    quarter = half // 2
    lines = planes * rows
    known = jnp.concatenate([explicit[...].reshape(lines, points), got[...]], axis=0)
    solved = split_dot(split(matrix[...]), split(known))
    sides = (solved[:, :half] + solved[:, half:], solved[:, :half] - solved[:, half:])
    periods = []
    for parity in range(2):
        table = (azimuth[parity, 0], azimuth[parity, 1])
        spectrum = split_dot(split(sides[parity]), table).reshape(planes, rows, half)
        swapped = jnp.concatenate([spectrum[..., quarter:], spectrum[..., :quarter]], axis=-1)
        smooth = spectrum * filters[:, parity * half : (parity + 1) * half]
        slope = swapped * filters[:, points + parity * half : points + (parity + 1) * half]
        both = jnp.concatenate([smooth, slope], axis=0).reshape(2 * planes * rows, half)
        periods.append(split_dot(split(both), table, 1).reshape(2, planes, rows, half))
    for side in range(2):
        where = slice(side * half, (side + 1) * half)
        value = fade = None
        for plane in range(planes):
            even, odd = periods[0][:, plane], periods[1][:, plane]
            both = even + odd if side == 0 else even - odd
            courant = CZ * axial_rate[plane, :, where]
            inverse_rate = 1.0 / (1.0 + courant)
            factor = courant * inverse_rate
            scaled = inverse_rate * (both[0] - swirl_rate[plane, :, where] * both[1])
            value = scaled if plane == 0 else factor * value + scaled
            fade = factor if plane == 0 else factor * fade
            partial[plane, :, where] = value
            decay[plane, :, where] = fade
        if other is None:
            mine[:, where] = value
            continue
        is_mine = lax.axis_index("ax") % 2 == side
        for index, last in enumerate((value, fade)[: mine.shape[0]]):

            @pl.when(is_mine)
            def _():
                mine[index] = last

            @pl.when(jnp.logical_not(is_mine))
            def _():
                other[index] = last


def ends_kernel(field, pair, chain):
    planes = field.shape[0]
    odd = lax.axis_index("ax") % 2 == 1
    for j in range(HALO):
        low, high = field[j], field[planes - HALO + j]
        pair[j] = jnp.where(odd, low, high)
        chain[j] = jnp.where(odd, high, low)


def chip_kernel(mine, got, block, behind, spans):
    odd = lax.axis_index("ax") % 2 == 1
    value0, value1 = jnp.where(odd, got[0], mine[0]), jnp.where(odd, mine[0], got[0])
    span0, span1 = jnp.where(odd, got[1], mine[1]), jnp.where(odd, mine[1], got[1])
    block[0] = value1 + span1 * value0
    block[1] = span0 * span1
    behind[...] = value0
    spans[0], spans[1] = span0, span1


def couple_kernel(block, got, joint, prefix, before):
    upper = (lax.axis_index("ax") // 2) % 2 == 1
    keep = jnp.where(upper, 1.0, got[1])
    take = jnp.where(upper, block[1], 1.0)
    joint[0] = keep * block[0] + take * got[0]
    joint[1] = block[1] * got[1]
    prefix[...] = jnp.where(upper, got[0], 0.0)
    before[...] = jnp.where(upper, got[1], 1.0)


def enter_kernel(got1, got2, got3, prefix, before, behind, spans, mine, packed):
    place = lax.axis_index("ax")
    odd = place % 2 == 1
    quad = place // 4
    near = before[...]
    weight1 = jnp.where(quad % 2 == 1, near, 0.0)
    weight2 = near * jnp.where(quad == 2, got3[1], jnp.where(quad == 3, got1[1], 0.0))
    weight3 = near * jnp.where(quad == 2, 1.0, jnp.where(quad == 3, got1[1] * got2[1], 0.0))
    into0 = prefix[...] + weight1 * got1[0] + weight2 * got2[0] + weight3 * got3[0]
    into1 = spans[0] * into0 + behind[...]
    mine[...] = jnp.where(odd, into1, into0)
    packed[0] = jnp.where(odd, into0, into1)
    start = near * jnp.where(quad % 2 == 1, got1[1], 1.0)
    start = start * jnp.where(quad >= 2, got2[1] * got3[1], 1.0)
    packed[1] = start
    packed[2] = 1.0 / (start * (spans[0] * spans[1]))
    packed[3], packed[4] = spans[0], spans[1]


def widen_kernel(packed, got, scales):
    half = packed.shape[2]
    odd = lax.axis_index("ax") % 2 == 1
    for index in range(scales.shape[0]):
        for side in range(2):
            own = odd == (side == 1)
            value = jnp.where(own, packed[index + 1], got[index + 1])
            scales[index, :, side * half : (side + 1) * half] = value


def chip_again_kernel(total, got, scales, sent):
    odd = lax.axis_index("ax") % 2 == 1
    value0 = jnp.where(odd, got[...], total[...])
    value1 = jnp.where(odd, total[...], got[...])
    sent[...] = (value1 + scales[3] * value0) * scales[1]


def gather_kernel(far0, far1, far2, far3, below):
    place = lax.axis_index("ax")
    odd = place % 2 == 1
    chip = place // 2
    total = jnp.zeros_like(below)
    for far, (mask1, mask0) in zip((far0, far1, far2, far3), FAR):
        take = chip ^ jnp.where(odd, mask1, mask0) < chip
        if mask0 == FAR[0][0]:
            take = jnp.logical_and(take, odd)
        total = total + jnp.where(take, far[...], 0.0)
    below[...] = total


def finish_kernel(partial, decay, mine, got, field, pair, chain):
    planes, rows, points = partial.shape
    half = points // 2
    odd = lax.axis_index("ax") % 2 == 1
    for side in range(2):
        where = slice(side * half, (side + 1) * half)
        incoming = jnp.where(odd == (side == 1), mine[...], got[0])
        ends = {}
        for plane in range(planes):
            value = partial[plane, :, where] + decay[plane, :, where] * incoming
            field[plane, :, where] = value
            ends[plane] = value
        for j in range(HALO):
            low, high = ends[j], ends[planes - HALO + j]
            pair[j, :, where] = jnp.where(odd, low, high)
            chain[j, :, where] = jnp.where(odd, high, low)


def last_kernel(partial, decay, below, got, total, before, scales, out, field, sems):
    planes = partial.shape[0]
    odd = lax.axis_index("ax") % 2 == 1
    into0 = scales[0] * (below[...] + got[...])
    value0 = jnp.where(odd, before[...], total[...])
    incoming = jnp.where(odd, scales[2] * into0 + value0, into0)
    copies = []
    for plane in range(planes):
        field[plane] = partial[plane] + decay[plane] * incoming
        if plane % 2 == 1:
            pair = pl.ds(plane - 1, 2)
            copy = pltpu.make_async_copy(field.at[pair], out.at[pair], sems.at[plane // 2])
            copy.start()
            copies.append(copy)
    for copy in copies:
        copy.wait()


def call(kernel, out_shape, *args, vmem=4):
    return pl.pallas_call(
        kernel,
        out_shape=out_shape,
        in_specs=[pl.BlockSpec(memory_space=pltpu.VMEM)] * len(args),
        out_specs=jax.tree.map(lambda _: pl.BlockSpec(memory_space=pltpu.VMEM), out_shape),
        compiler_params=pltpu.CompilerParams(vmem_limit_bytes=vmem * 1024 * 1024),
    )(*args)


def body(scalar, axial_rate, swirl_rate):
    planes, rows, points = scalar.shape
    half = points // 2
    groups = lax.axis_size("xs")
    lines = planes * rows
    tables = azimuth_tables(points)
    azimuth = jnp.asarray(np.stack([np.stack(split_bf16(t)) for t in tables]))
    radial = radial_tables(rows * groups, groups, planes)
    damping = filter_tables(rows * groups, points).reshape(groups, rows, 2 * points)

    def shape(*sizes):
        return jax.ShapeDtypeStruct(sizes, jnp.float32)

    block, ends, one = shape(planes, rows, points), shape(HALO, rows, points), shape(rows, half)

    pair_end, chain_end = call(ends_kernel, (ends, ends), scalar)
    chain, pair = chain_swap(chain_end), swap(pair_end, 1)
    inner = call(inner_kernel, block, scalar)
    matrix, edges, filters = pl.pallas_call(
        setup_kernel,
        out_shape=(
            shape(lines, lines + groups * planes),
            shape(2 * planes, lines),
            shape(rows, 2 * points),
        ),
        in_specs=[pl.BlockSpec(memory_space=pltpu.HBM)] * 2,
        out_specs=(pl.BlockSpec(memory_space=pltpu.VMEM),) * 3,
        scratch_shapes=[pltpu.SemaphoreType.DMA((3,))],
        compiler_params=pltpu.CompilerParams(vmem_limit_bytes=4 * 1024 * 1024),
    )(jnp.asarray(radial), jnp.asarray(damping))

    for substep in range(SUBSTEPS):
        explicit, sent = call(
            carry_kernel, (block, shape(groups, planes, points)), inner, pair, chain, edges
        )
        got = lax.all_to_all(sent, "xs", split_axis=0, concat_axis=0, tiled=True)
        first = substep == 0
        parts, plane = shape(2, rows, half), shape(rows, points)
        partial, decay, *sides = call(
            middle_kernel,
            (block, block, parts, parts) if first else (block, block, plane),
            explicit,
            got.reshape(groups * planes, points),
            matrix,
            azimuth,
            filters,
            axial_rate,
            swirl_rate,
            vmem=16,
        )
        if first:
            mine, other = sides
            out = (parts, one, parts)
            value, behind, spans = call(chip_kernel, out, mine, swap(other, 1))
            value, prefix, before = call(couple_kernel, (parts, one, one), value, swap(value, 2))
            far3, far2, far1 = swap(value, 12), swap(value, 8), swap(value, 4)
            out = (one, shape(5, rows, half))
            mine, packed = call(
                enter_kernel, out, far1, far2, far3, prefix, before, behind, spans
            )
            got = swap(packed, 1)
            field, pair_end, chain_end = call(
                finish_kernel, (block, ends, ends), partial, decay, mine, got
            )
            chain, pair = chain_swap(chain_end), swap(pair_end, 1)
            inner = call(inner_kernel, block, field)
            scales = call(widen_kernel, shape(4, rows, points), packed, got)
        else:
            (total,) = sides
            before = swap(total, 1)
            sent = call(chip_again_kernel, plane, total, before, scales)
            below = call(gather_kernel, plane, *(far_swap(sent, masks) for masks in FAR))
            got = swap(below, 1)
    return pl.pallas_call(
        last_kernel,
        out_shape=block,
        in_specs=[pl.BlockSpec(memory_space=pltpu.VMEM)] * 7,
        out_specs=pl.BlockSpec(memory_space=pl.ANY),
        scratch_shapes=[
            pltpu.VMEM((planes, rows, points), jnp.float32),
            pltpu.SemaphoreType.DMA((planes // 2,)),
        ],
        compiler_params=pltpu.CompilerParams(vmem_limit_bytes=4 * 1024 * 1024),
    )(partial, decay, below, got, total, before, scales)


def solution(mesh):
    return jax.shard_map(
        body,
        mesh=mesh,
        in_specs=(P("ax", "xs", None), P("ax", "xs", None), P("ax", "xs", None)),
        out_specs=P("ax", "xs", None),
        check_vma=False,
    )
```

```python
import math

import jax
import jax.numpy as jnp
import ml_dtypes
import numpy as np
from jax import lax
from jax.experimental import pallas as pl
from jax.experimental.pallas import tpu as pltpu
from jax.sharding import PartitionSpec as P

CZ = 8
SUBSTEPS = 2
AXIAL_WEIGHT = 0.2
AZIMUTH_DAMP = 0.5
DIFFUSION = 1.0
STENCIL = (
    -1.0 / 560.0,
    8.0 / 315.0,
    -0.2,
    1.6,
    -205.0 / 72.0,
    1.6,
    -0.2,
    8.0 / 315.0,
    -1.0 / 560.0,
)
HALO = 4
FAR = ((4, 6), (5, 2), (3, 7), (7, 1))


def split_bf16(table):
    high = table.astype(ml_dtypes.bfloat16)
    low = (table - high.astype(np.float64)).astype(ml_dtypes.bfloat16)
    return high, low


def radial_tables(cells, groups, planes):
    rows = cells // groups
    index = np.arange(cells, dtype=np.float64)
    radius = index + 0.5
    upper = np.where(index < cells - 1, index + 1.0, 0.0)
    sub = -DIFFUSION * index / radius
    sup = -DIFFUSION * upper / radius
    matrix = np.diag(1.0 - sub - sup) + np.diag(sub[1:], -1) + np.diag(sup[:-1], 1)
    green = np.linalg.inv(matrix)
    diag = np.diag(green)
    down = np.diag(green, -1) / diag[:-1]
    up = np.diag(green, 1) / diag[1:]
    same = np.eye(planes)
    lines = planes * rows
    out = np.zeros((groups, lines + 2 * planes, lines + groups * planes), np.float32)
    for g in range(groups):
        first, last = g * rows, g * rows + rows - 1
        block = green[first : last + 1, first : last + 1]
        join = np.zeros((rows, groups))
        for i in range(rows):
            for source in range(groups):
                if source < g:
                    join[i, source] = np.prod(down[source * rows + rows - 1 : first + i])
                elif source > g:
                    join[i, source] = np.prod(up[first + i : source * rows])
        out[g, :lines, :lines] = np.kron(same, block)
        out[g, :lines, lines:] = np.einsum("zy,is->zisy", same, join).reshape(lines, -1)
        out[g, lines : lines + planes, :lines] = np.kron(same, block[-1:])
        out[g, lines + planes :, :lines] = np.kron(same, block[:1])
    return out


def azimuth_tables(points):
    half = points // 2
    quarter = half // 2
    grid = np.arange(half)
    out = []
    for parity in range(2):
        wave = 2 * np.arange(quarter) + parity
        angle = ((grid[:, None] * wave[None, :]) % points) * (2.0 * math.pi / points)
        cosine, sine = np.cos(angle), np.sin(angle)
        if parity == 0:
            sine[:, 0] = np.where(grid % 2 == 0, 1.0, -1.0)
        out.append(np.concatenate([cosine, sine], axis=1))
    return out


def filter_tables(cells, points):
    half = points // 2
    quarter = half // 2
    radius = np.arange(cells) + 0.5
    out = []
    for parity in range(2):
        wave = np.tile(2.0 * np.arange(quarter) + parity, 2)
        rate = wave * (2.0 * math.pi / points)
        weight = np.full(half, 2.0 / points)
        sign = np.repeat([1.0, -1.0], quarter)
        if parity == 0:
            wave[quarter] = half
            weight[0] = weight[quarter] = 1.0 / points
        damp = 1.0 / (1.0 + AZIMUTH_DAMP * wave[None, :] ** 2 / radius[:, None] ** 2)
        out.append((damp * weight, damp * (sign * rate * (2.0 / points))))
    table = [out[0][0], out[1][0], out[0][1], out[1][1]]
    return np.concatenate(table, axis=1).astype(np.float32)


def swap(value, mask):
    count = lax.axis_size("ax")
    return lax.ppermute(value, "ax", [(i, i ^ mask) for i in range(count)])


def far_swap(value, masks):
    count = lax.axis_size("ax")
    return lax.ppermute(value, "ax", [(i, i ^ 2 * masks[1 - i % 2]) for i in range(count)])


def chain_swap(value):
    count = lax.axis_size("ax")
    pairs = [(i, (i + 1) % count if i % 2 else (i - 1) % count) for i in range(count)]
    return lax.ppermute(value, "ax", pairs)


def split(values):
    coarse = values.astype(jnp.bfloat16)
    return coarse, (values - coarse.astype(jnp.float32)).astype(jnp.bfloat16)


def split_dot(left, right, depth=0):
    def dot(x, y):
        return lax.dot_general(
            x, y, (((1,), (depth,)), ((), ())), preferred_element_type=jnp.float32
        )

    return dot(left[0], right[0]) + (dot(left[1], right[0]) + dot(left[0], right[1]))


def setup_kernel(radial, damping, matrix, edges, filters, sems):
    group = lax.axis_index("xs")
    lines, columns = matrix.shape[0], edges.shape[1]
    copies = [
        pltpu.make_async_copy(
            radial.at[group, pl.ds(lines, edges.shape[0]), pl.ds(0, columns)], edges, sems.at[0]
        ),
        pltpu.make_async_copy(radial.at[group, pl.ds(0, lines)], matrix, sems.at[1]),
        pltpu.make_async_copy(damping.at[group], filters, sems.at[2]),
    ]
    for copy in copies:
        copy.start()
    for copy in copies:
        copy.wait()


def inner_kernel(field, inner):
    planes = field.shape[0]
    for plane in range(planes):
        value = (1.0 + AXIAL_WEIGHT * STENCIL[HALO]) * field[plane]
        for source in range(max(0, plane - HALO), min(planes, plane + HALO + 1)):
            if source != plane:
                value = value + (AXIAL_WEIGHT * STENCIL[HALO + source - plane]) * field[source]
        inner[plane] = value


def carry_kernel(inner, pair, chain, edges, explicit, sent):
    planes, rows, points = inner.shape
    groups = sent.shape[0]
    place = lax.axis_index("ax")
    group = lax.axis_index("xs")
    odd = place % 2 == 1
    low_scale = jnp.where(place > 0, 1.0, 0.0)
    high_scale = jnp.where(place < lax.axis_size("ax") - 1, 1.0, 0.0)
    quarter = points // 4
    for part in range(4):
        where = slice(part * quarter, (part + 1) * quarter)
        low = [jnp.where(odd, pair[j, :, where], chain[j, :, where]) for j in range(HALO)]
        high = [jnp.where(odd, chain[j, :, where], pair[j, :, where]) for j in range(HALO)]
        low = [low_scale * value for value in low]
        high = [high_scale * value for value in high]
        for plane in range(planes):
            value = inner[plane, :, where]
            for j in range(HALO):
                if plane + HALO - j <= HALO:
                    value = value + (AXIAL_WEIGHT * STENCIL[j - plane]) * low[j]
                if planes + j - plane <= HALO:
                    value = value + (AXIAL_WEIGHT * STENCIL[HALO + planes + j - plane]) * high[j]
            explicit[plane, :, where] = value
    lines = explicit[...].reshape(planes * rows, points)
    carry = split_dot(split(edges[...]), split(lines))
    for target in range(groups):
        sent[target] = jnp.where(target > group, carry[:planes], carry[planes:])


def middle_kernel(
    explicit,
    got,
    matrix,
    azimuth,
    filters,
    axial_rate,
    swirl_rate,
    partial,
    decay,
    mine,
    other=None,
):
    planes, rows, points = partial.shape
    half = points // 2
    quarter = half // 2
    lines = planes * rows
    known = jnp.concatenate([explicit[...].reshape(lines, points), got[...]], axis=0)
    solved = split_dot(split(matrix[...]), split(known))
    sides = (solved[:, :half] + solved[:, half:], solved[:, :half] - solved[:, half:])
    periods = []
    for parity in range(2):
        table = (azimuth[parity, 0], azimuth[parity, 1])
        spectrum = split_dot(split(sides[parity]), table).reshape(planes, rows, half)
        swapped = jnp.concatenate([spectrum[..., quarter:], spectrum[..., :quarter]], axis=-1)
        smooth = spectrum * filters[:, parity * half : (parity + 1) * half]
        slope = swapped * filters[:, points + parity * half : points + (parity + 1) * half]
        both = jnp.concatenate([smooth, slope], axis=0).reshape(2 * planes * rows, half)
        periods.append(split_dot(split(both), table, 1).reshape(2, planes, rows, half))
    for side in range(2):
        where = slice(side * half, (side + 1) * half)
        value = fade = None
        for plane in range(planes):
            even, odd = periods[0][:, plane], periods[1][:, plane]
            both = even + odd if side == 0 else even - odd
            courant = CZ * axial_rate[plane, :, where]
            inverse_rate = 1.0 / (1.0 + courant)
            factor = courant * inverse_rate
            scaled = inverse_rate * (both[0] - swirl_rate[plane, :, where] * both[1])
            value = scaled if plane == 0 else factor * value + scaled
            fade = factor if plane == 0 else factor * fade
            partial[plane, :, where] = value
            decay[plane, :, where] = fade
        if other is None:
            mine[:, where] = value
            continue
        is_mine = lax.axis_index("ax") % 2 == side
        for index, last in enumerate((value, fade)[: mine.shape[0]]):

            @pl.when(is_mine)
            def _():
                mine[index] = last

            @pl.when(jnp.logical_not(is_mine))
            def _():
                other[index] = last


def ends_kernel(field, pair, chain):
    planes = field.shape[0]
    odd = lax.axis_index("ax") % 2 == 1
    for j in range(HALO):
        low, high = field[j], field[planes - HALO + j]
        pair[j] = jnp.where(odd, low, high)
        chain[j] = jnp.where(odd, high, low)


def chip_kernel(mine, got, block, behind, spans):
    odd = lax.axis_index("ax") % 2 == 1
    value0, value1 = jnp.where(odd, got[0], mine[0]), jnp.where(odd, mine[0], got[0])
    span0, span1 = jnp.where(odd, got[1], mine[1]), jnp.where(odd, mine[1], got[1])
    block[0] = value1 + span1 * value0
    block[1] = span0 * span1
    behind[...] = value0
    spans[0], spans[1] = span0, span1


def couple_kernel(block, got, joint, prefix, before):
    upper = (lax.axis_index("ax") // 2) % 2 == 1
    keep = jnp.where(upper, 1.0, got[1])
    take = jnp.where(upper, block[1], 1.0)
    joint[0] = keep * block[0] + take * got[0]
    joint[1] = block[1] * got[1]
    prefix[...] = jnp.where(upper, got[0], 0.0)
    before[...] = jnp.where(upper, got[1], 1.0)


def enter_kernel(got1, got2, got3, prefix, before, behind, spans, mine, packed):
    place = lax.axis_index("ax")
    odd = place % 2 == 1
    quad = place // 4
    near = before[...]
    weight1 = jnp.where(quad % 2 == 1, near, 0.0)
    weight2 = near * jnp.where(quad == 2, got3[1], jnp.where(quad == 3, got1[1], 0.0))
    weight3 = near * jnp.where(quad == 2, 1.0, jnp.where(quad == 3, got1[1] * got2[1], 0.0))
    into0 = prefix[...] + weight1 * got1[0] + weight2 * got2[0] + weight3 * got3[0]
    into1 = spans[0] * into0 + behind[...]
    mine[...] = jnp.where(odd, into1, into0)
    packed[0] = jnp.where(odd, into0, into1)
    start = near * jnp.where(quad % 2 == 1, got1[1], 1.0)
    start = start * jnp.where(quad >= 2, got2[1] * got3[1], 1.0)
    packed[1] = start
    packed[2] = 1.0 / (start * (spans[0] * spans[1]))
    packed[3], packed[4] = spans[0], spans[1]


def widen_kernel(packed, got, scales):
    half = packed.shape[2]
    odd = lax.axis_index("ax") % 2 == 1
    for index in range(scales.shape[0]):
        for side in range(2):
            own = odd == (side == 1)
            value = jnp.where(own, packed[index + 1], got[index + 1])
            scales[index, :, side * half : (side + 1) * half] = value


def chip_again_kernel(total, got, scales, sent):
    odd = lax.axis_index("ax") % 2 == 1
    value0 = jnp.where(odd, got[...], total[...])
    value1 = jnp.where(odd, total[...], got[...])
    sent[...] = (value1 + scales[3] * value0) * scales[1]


def gather_kernel(far0, far1, far2, far3, below):
    place = lax.axis_index("ax")
    odd = place % 2 == 1
    chip = place // 2
    total = jnp.zeros_like(below)
    for far, (mask1, mask0) in zip((far0, far1, far2, far3), FAR):
        take = chip ^ jnp.where(odd, mask1, mask0) < chip
        if mask0 in [masks[0] for masks in FAR]:
            take = jnp.logical_and(take, odd)
        total = total + jnp.where(take, far[...], 0.0)
    below[...] = total


def finish_kernel(partial, decay, mine, got, field, pair, chain):
    planes, rows, points = partial.shape
    half = points // 2
    odd = lax.axis_index("ax") % 2 == 1
    for side in range(2):
        where = slice(side * half, (side + 1) * half)
        incoming = jnp.where(odd == (side == 1), mine[...], got[0])
        ends = {}
        for plane in range(planes):
            value = partial[plane, :, where] + decay[plane, :, where] * incoming
            field[plane, :, where] = value
            ends[plane] = value
        for j in range(HALO):
            low, high = ends[j], ends[planes - HALO + j]
            pair[j, :, where] = jnp.where(odd, low, high)
            chain[j, :, where] = jnp.where(odd, high, low)


def last_kernel(partial, decay, below, got, total, before, scales, out, field, sems):
    planes = partial.shape[0]
    odd = lax.axis_index("ax") % 2 == 1
    into0 = scales[0] * (below[...] + got[...])
    value0 = jnp.where(odd, before[...], total[...])
    incoming = jnp.where(odd, scales[2] * into0 + value0, into0)
    copies = []
    for plane in range(planes):
        field[plane] = partial[plane] + decay[plane] * incoming
        if plane % 2 == 1:
            pair = pl.ds(plane - 1, 2)
            copy = pltpu.make_async_copy(field.at[pair], out.at[pair], sems.at[plane // 2])
            copy.start()
            copies.append(copy)
    for copy in copies:
        copy.wait()


def call(kernel, out_shape, *args, vmem=4):
    return pl.pallas_call(
        kernel,
        out_shape=out_shape,
        in_specs=[pl.BlockSpec(memory_space=pltpu.VMEM)] * len(args),
        out_specs=jax.tree.map(lambda _: pl.BlockSpec(memory_space=pltpu.VMEM), out_shape),
        compiler_params=pltpu.CompilerParams(vmem_limit_bytes=vmem * 1024 * 1024),
    )(*args)


def body(scalar, axial_rate, swirl_rate):
    planes, rows, points = scalar.shape
    half = points // 2
    groups = lax.axis_size("xs")
    lines = planes * rows
    tables = azimuth_tables(points)
    azimuth = jnp.asarray(np.stack([np.stack(split_bf16(t)) for t in tables]))
    radial = radial_tables(rows * groups, groups, planes)
    damping = filter_tables(rows * groups, points).reshape(groups, rows, 2 * points)

    def shape(*sizes):
        return jax.ShapeDtypeStruct(sizes, jnp.float32)

    block, ends, one = shape(planes, rows, points), shape(HALO, rows, points), shape(rows, half)

    pair_end, chain_end = call(ends_kernel, (ends, ends), scalar)
    chain, pair = chain_swap(chain_end), swap(pair_end, 1)
    inner = call(inner_kernel, block, scalar)
    matrix, edges, filters = pl.pallas_call(
        setup_kernel,
        out_shape=(
            shape(lines, lines + groups * planes),
            shape(2 * planes, lines),
            shape(rows, 2 * points),
        ),
        in_specs=[pl.BlockSpec(memory_space=pltpu.HBM)] * 2,
        out_specs=(pl.BlockSpec(memory_space=pltpu.VMEM),) * 3,
        scratch_shapes=[pltpu.SemaphoreType.DMA((3,))],
        compiler_params=pltpu.CompilerParams(vmem_limit_bytes=4 * 1024 * 1024),
    )(jnp.asarray(radial), jnp.asarray(damping))

    for substep in range(SUBSTEPS):
        explicit, sent = call(
            carry_kernel, (block, shape(groups, planes, points)), inner, pair, chain, edges
        )
        got = lax.all_to_all(sent, "xs", split_axis=0, concat_axis=0, tiled=True)
        first = substep == 0
        parts, plane = shape(2, rows, half), shape(rows, points)
        partial, decay, *sides = call(
            middle_kernel,
            (block, block, parts, parts) if first else (block, block, plane),
            explicit,
            got.reshape(groups * planes, points),
            matrix,
            azimuth,
            filters,
            axial_rate,
            swirl_rate,
            vmem=16,
        )
        if first:
            mine, other = sides
            out = (parts, one, parts)
            value, behind, spans = call(chip_kernel, out, mine, swap(other, 1))
            value, prefix, before = call(couple_kernel, (parts, one, one), value, swap(value, 2))
            far3, far2, far1 = swap(value, 12), swap(value, 8), swap(value, 4)
            out = (one, shape(5, rows, half))
            mine, packed = call(
                enter_kernel, out, far1, far2, far3, prefix, before, behind, spans
            )
            got = swap(packed, 1)
            field, pair_end, chain_end = call(
                finish_kernel, (block, ends, ends), partial, decay, mine, got
            )
            chain, pair = chain_swap(chain_end), swap(pair_end, 1)
            inner = call(inner_kernel, block, field)
            scales = call(widen_kernel, shape(4, rows, points), packed, got)
        else:
            (total,) = sides
            before = swap(total, 1)
            sent = call(chip_again_kernel, plane, total, before, scales)
            below = call(gather_kernel, plane, *(far_swap(sent, masks) for masks in FAR))
            got = swap(below, 1)
    return pl.pallas_call(
        last_kernel,
        out_shape=block,
        in_specs=[pl.BlockSpec(memory_space=pltpu.VMEM)] * 7,
        out_specs=pl.BlockSpec(memory_space=pl.ANY),
        scratch_shapes=[
            pltpu.VMEM((planes, rows, points), jnp.float32),
            pltpu.SemaphoreType.DMA((planes // 2,)),
        ],
        compiler_params=pltpu.CompilerParams(vmem_limit_bytes=4 * 1024 * 1024),
    )(partial, decay, below, got, total, before, scales)


def solution(mesh):
    return jax.shard_map(
        body,
        mesh=mesh,
        in_specs=(P("ax", "xs", None), P("ax", "xs", None), P("ax", "xs", None)),
        out_specs=P("ax", "xs", None),
        check_vma=False,
    )
```
